512 devices in a mesh: replica: 64 (over x, y, core), tensor: 8 (over z).
Axes of the slice: x: 4, y: 8, z: 8, core: 2. Of those that a mesh axis runs over, the one named last changes fastest.
Arguments:
- queries: bfloat16 [8192, 4096], P('replica', 'tensor'), may hold values from -9 to 9
- new_kv: bfloat16 [2, 8192, 1024], P(None, 'replica', 'tensor'), may hold values from -16 to 16
- cache: bfloat16 [512, 2, 64, 1024], P('replica', None, None, 'tensor'), may hold values from -16 to 16
- block_owner: int32 [64, 64], replicated, may hold values from 0 to 63, as said below
- block_slot: int32 [64, 64], replicated, may hold values from 0 to 7, as said below
- prefix_blocks: int32 [64], replicated, may hold values from 1 to 64, 2048 in all
- out_weight: bfloat16 [4096, 4096], P('tensor'), may hold values from -0.09375 to 0.09375
Outputs:
- mixed: bfloat16 [8192, 4096], P(('replica', 'tensor'))
The draws below stay inside these ranges and needn't reach their ends.
Inputs may be any that keep to these rules, and one draw needn't show every extreme that they name: `block_owner`: within one replica's row, every owner that appears does so exactly 2 times. `block_slot`: the 2 entries of one replica's row that name one owner name different slots. `prefix_blocks`: the largest is 64 in every draw.
All inputs are finite; a program needn't handle non-finite values.
Results may differ from the reference program's by a relative error of at most 0.024.
Values may be sent and summed in bfloat16 or wider, within the bound.
No kernel may reach another device: no remote copies, remote signals or barrier semaphores. Data moves between devices by JAX's collectives and lax.ppermute only.
A program may use at most 64 MiB of HBM per device.

```python
import math
import jax
import jax.numpy as jnp
import numpy as np
from jax import lax

HQ = 32
KVH = 8
HD = 128
DW = 4096
BLOCK = 64
MAXB = 64
SLOTS = 8
TOK = 128
CAP = 2
TOKENS = 8192
POOL = 512
N_REPLICA = 64
N_TENSOR = 8


def value_scales(key, shape):
    return jnp.exp(jax.random.uniform(key, shape, jnp.float32, math.log(0.3), math.log(3.0)))


def table_pair(key):
    groups = MAXB // CAP

    def one_row(row_key):
        owner_key, slot_key, order_key = jax.random.split(row_key, 3)
        owners = jax.random.permutation(owner_key, N_REPLICA)[:groups].astype(jnp.int32)
        ranking = jax.random.randint(slot_key, (groups, SLOTS), 0, 1 << 20) * SLOTS + jnp.arange(SLOTS, dtype=jnp.int32)[None, :]
        slot_ids = jnp.argsort(ranking, axis=1, stable=True)[:, :CAP].astype(jnp.int32)
        order = jax.random.permutation(order_key, MAXB)
        return (jnp.repeat(owners, CAP)[order], slot_ids.reshape(-1)[order])
    return jax.vmap(one_row)(jax.random.split(key, N_REPLICA))


def draw_queries(key, part):
    key = jax.random.fold_in(key, 11)
    shape = (N_REPLICA, TOK // 32, 32, HQ, HD)
    base = jnp.clip(3.0 * jax.random.normal(key, shape, jnp.float32), -9.0, 9.0)
    return base.reshape(TOKENS, HQ * HD).astype(jnp.bfloat16)


def draw_new_kv(key, part):
    key = jax.random.fold_in(key, 12)
    key_part, value_part, scale_part = jax.random.split(key, 3)
    shape = (N_REPLICA, TOK // 32, 32, KVH, HD)
    scales = value_scales(scale_part, (N_REPLICA, TOK // 32, 32, KVH, 1))
    key_rows = jnp.clip(jax.random.normal(key_part, shape, jnp.float32), -5.0, 5.0)
    value_rows = jnp.clip(jax.random.normal(value_part, shape, jnp.float32), -5.0, 5.0) * scales
    return jnp.stack([key_rows, value_rows]).reshape(2, TOKENS, KVH * HD).astype(jnp.bfloat16)


def draw_cache(key, part):
    key = jax.random.fold_in(key, 13)
    key_part, value_part, scale_part = jax.random.split(key, 3)
    shape = (POOL, BLOCK, KVH, HD)
    scales = value_scales(scale_part, (POOL, BLOCK, KVH, 1))
    key_rows = jnp.clip(jax.random.normal(key_part, shape, jnp.float32), -5.0, 5.0)
    value_rows = jnp.clip(jax.random.normal(value_part, shape, jnp.float32), -5.0, 5.0) * scales
    return jnp.stack([key_rows, value_rows], axis=1).reshape(POOL, 2, BLOCK, KVH * HD).astype(jnp.bfloat16)


def draw_block_owner(key, part):
    owners, slot_ids = table_pair(key)
    return owners.astype(jnp.int32)


def draw_block_slot(key, part):
    owners, slot_ids = table_pair(key)
    return slot_ids.astype(jnp.int32)


def levels(key, dims, cuts, low, high):
    level, own = 1.0, jax.random.fold_in(key, 6)
    for position, blocks in cuts:
        draws = jnp.exp(jax.random.uniform(jax.random.fold_in(own, position), (blocks,), jnp.float32, low / len(cuts), high / len(cuts)))
        level = level * jnp.repeat(draws, dims[position] // blocks).reshape([-1 if axis == position else 1 for axis in range(len(dims))])
    return level


def length_profile(count, total, most, slope):
    portions = [(1 << 20) // math.isqrt(rank ** slope) + 1 for rank in range(2, count + 1)]
    spare, counts = total - most - (count - 1), [1] * (count - 1)
    while spare > 0:
        candidates = [i for i in range(count - 1) if counts[i] < most]
        mass, left = sum([portions[i] for i in candidates]), spare
        for i in candidates:
            addition = min(most - counts[i], max(1, left * portions[i] // mass), spare)
            counts[i] = counts[i] + addition
            spare = spare - addition
    return np.array([most] + counts)


def uneven(rng, count, total, reach, slope):
    if count == 2:
        one = jax.random.randint(rng, (), max(1, total - reach), min(reach, total - 1) + 1)
        return jnp.stack([one, total - one])
    sizes = jnp.asarray(length_profile(count, total, reach, slope), jnp.int32)
    twos = (count - 1) // 2
    donor, taker = sizes[1:1 + 2 * twos:2], sizes[2:2 + 2 * twos:2]
    slack = jnp.minimum(donor - 1, reach - taker)
    passed = jax.random.randint(jax.random.fold_in(rng, 1), (twos,), 0, 1 << 20) % (slack + 1)
    sizes = sizes.at[1:1 + 2 * twos:2].set(donor - passed).at[2:2 + 2 * twos:2].set(taker + passed)
    return sizes[jax.random.permutation(jax.random.fold_in(rng, 2), count)]


def centred(rng, dims, deviation, limit, shards=(), kind=jnp.bfloat16):
    values = jax.random.normal(rng, dims, jnp.float32) * deviation
    if len(shards) > 0:
        values = levels(rng, dims, shards, -0.22, 0.18) * values
    return jnp.clip(values, min=-limit, max=limit).astype(kind)


def setup_inputs(seed: int = 0) -> dict:
    seeds = jax.random.split(jax.random.key(seed), 8)
    queries = draw_queries(jax.random.fold_in(seeds[7], 71), 0)
    new_kv = draw_new_kv(jax.random.fold_in(seeds[7], 71), 0)
    cache = draw_cache(jax.random.fold_in(seeds[7], 71), 0)
    block_owner = draw_block_owner(jax.random.fold_in(seeds[7], 71), 0)
    block_slot = draw_block_slot(jax.random.fold_in(seeds[7], 71), 0)
    prefix_blocks = uneven(seeds[5], N_REPLICA, N_REPLICA * MAXB // 2, MAXB, 2).astype(jnp.int32)
    out_weight = centred(seeds[6], (HQ * HD, DW), (HQ * HD) ** -0.5, 0.09375, ((0, 8),))
    return {"queries": queries, "new_kv": new_kv, "cache": cache, "block_owner": block_owner, "block_slot": block_slot, "prefix_blocks": prefix_blocks, "out_weight": out_weight}


def reference(queries, new_kv, cache, block_owner, block_slot, prefix_blocks, out_weight):
    per_group = HQ // KVH
    scaling = HD ** -0.5
    prefix_len = MAXB * BLOCK
    weight_full = out_weight.astype(jnp.float32).reshape(N_TENSOR, HQ * HD // N_TENSOR, DW)

    def one_replica(replica):
        first_row = replica * TOK
        query_rows = lax.dynamic_slice_in_dim(queries, first_row, TOK, 0).astype(jnp.float32)
        query_rows = query_rows.reshape(TOK, KVH, per_group, HD)
        fresh = lax.dynamic_slice_in_dim(new_kv, first_row, TOK, 1)
        owners = lax.dynamic_index_in_dim(block_owner, replica, 0, keepdims=False)
        slot_ids = lax.dynamic_index_in_dim(block_slot, replica, 0, keepdims=False)
        blocks = cache[(owners * SLOTS + slot_ids).astype(jnp.int32)]
        key_rows = jnp.concatenate([blocks[:, 0].reshape(prefix_len, KVH * HD), fresh[0]], axis=0)
        key_rows = key_rows.astype(jnp.float32).reshape(prefix_len + TOK, KVH, HD)
        value_rows = jnp.concatenate([blocks[:, 1].reshape(prefix_len, KVH * HD), fresh[1]], axis=0)
        value_rows = value_rows.astype(jnp.float32).reshape(prefix_len + TOK, KVH, HD)
        scores = jnp.einsum("tkgd,skd->kgts", query_rows, key_rows) * scaling
        places = jnp.arange(prefix_len + TOK, dtype=jnp.int32)
        row_ids = jnp.arange(TOK, dtype=jnp.int32)
        length = lax.dynamic_index_in_dim(prefix_blocks, replica, 0, keepdims=False)
        allowed = jnp.where(places[None, :] < prefix_len,
                            places[None, :] < length * BLOCK,
                            places[None, :] - prefix_len <= row_ids[:, None])
        scores = jnp.where(allowed[None, None], scores, -jnp.inf)
        highest = jnp.max(scores, axis=3, keepdims=True)
        weights = jnp.exp(scores - highest)
        totals = jnp.sum(weights, axis=3)
        rounded = lax.optimization_barrier(weights.astype(jnp.bfloat16)).astype(jnp.float32)
        attended = jnp.einsum("kgts,skd->tkgd", rounded, value_rows) / jnp.transpose(totals, (2, 0, 1))[..., None]
        attended = attended.reshape(TOK, N_TENSOR, HQ * HD // N_TENSOR).astype(jnp.bfloat16)
        partials = jnp.einsum("tgc,gcn->gtn", attended.astype(jnp.float32), weight_full)
        partials = lax.optimization_barrier(partials.astype(jnp.bfloat16)).astype(jnp.float32)
        return jnp.sum(partials, axis=0).astype(jnp.bfloat16)

    mixed = lax.map(one_replica, jnp.arange(N_REPLICA, dtype=jnp.int32))
    return mixed.reshape(N_REPLICA * TOK, DW)
```

```python
import math

import jax
import jax.numpy as jnp
from jax import lax
from jax.experimental import pallas as pl
from jax.experimental.pallas import tpu as pltpu
from jax.sharding import Mesh, PartitionSpec as P

HQ = 32
KVH = 8
HD = 128
BLOCK = 64
MAXB = 64
NX, NY, NC, NZ = 4, 8, 2, 8
GROUP = NX * NC
PER = HQ // KVH
TOK = 128
ROWS = PER * TOK
SLOTS = 8
CAP = 2
LIST = NY * CAP
TILE = 4
STATS = 16
NEGATIVE = -1e30
LOG2 = HD ** (-0.5) * math.log2(math.e)


def contract(a, b, da, db):
    return lax.dot_general(a, b, (((da,), (db,)), ((), ())), preferred_element_type=jnp.float32)


def attend_kernel(lists, own, queries, new_kv, *rest):
    shards, out, held, peak, total, weighted, sems = rest[:NY], *rest[NY:]
    copies = [pltpu.make_async_copy(shards[s], held.at[pl.ds(s * SLOTS, SLOTS)], sems.at[s]) for s in range(NY)]
    for copy in copies:
        copy.start()
    for copy in copies:
        copy.wait()

    def heads(g):
        q = queries[g]
        return jnp.concatenate([q[:, h * HD:(h + 1) * HD] for h in range(PER)], axis=0)

    def fold(scores, values):
        top = jnp.maximum(peak[...], jnp.max(scores, axis=0, keepdims=True))
        factor = jnp.exp2((peak[...] - top) * LOG2)
        weights = jnp.exp2((scores - top) * LOG2)
        peak[...] = top
        total[...] = total[...] * factor + jnp.sum(weights, axis=0, keepdims=True)
        weighted[...] = weighted[...] * factor + contract(values, weights.astype(jnp.bfloat16), 0, 0)

    def one_replica(g, carry):
        count = lists[g, LIST]
        peak[...] = jnp.full_like(peak, NEGATIVE)
        total[...] = jnp.zeros_like(total)
        weighted[...] = jnp.zeros_like(weighted)

        @pl.when(g == own[0])
        def _():
            scores = contract(new_kv[0], heads(g), 1, 1)
            key = lax.broadcasted_iota(jnp.int32, (TOK, ROWS), 0)
            token = lax.broadcasted_iota(jnp.int32, (TOK, ROWS), 1) % TOK
            fold(jnp.where(key <= token, scores, NEGATIVE), new_kv[1])

        def one_tile(i, carry):
            ids = [lists[g, i * TILE + k] for k in range(TILE)]
            keys = jnp.concatenate([held[b, 0] for b in ids], axis=0)
            values = jnp.concatenate([held[b, 1] for b in ids], axis=0)
            scores = contract(keys, heads(g), 1, 1)
            place = lax.broadcasted_iota(jnp.int32, scores.shape, 0)
            fold(jnp.where(place < (count - i * TILE) * BLOCK, scores, NEGATIVE), values)
            return carry

        lax.fori_loop(0, (count + TILE - 1) // TILE, one_tile, 0)
        filled = total[...] > 0.0
        safe = jnp.where(filled, total[...], 1.0)
        out[g, pl.ds(0, HD), :] = (weighted[...] / safe).astype(jnp.bfloat16)
        level = jnp.where(filled, peak[...] * LOG2 + jnp.log2(safe), NEGATIVE)
        first = level.astype(jnp.bfloat16)
        level = level - first.astype(jnp.float32)
        second = level.astype(jnp.bfloat16)
        third = level - second.astype(jnp.float32)
        row = lax.broadcasted_iota(jnp.int32, (STATS, ROWS), 0)
        stats = jnp.where(row == 0, first.astype(jnp.float32), jnp.where(row == 1, second.astype(jnp.float32), jnp.where(row == 2, third, 0.0)))
        out[g, pl.ds(HD, STATS), :] = stats.astype(jnp.bfloat16)
        return carry

    lax.fori_loop(0, GROUP, one_replica, 0)


def attend(lists, own, queries, new_kv, shards):
    vmem, smem = pl.BlockSpec(memory_space=pltpu.VMEM), pl.BlockSpec(memory_space=pltpu.SMEM)
    return pl.pallas_call(
        attend_kernel,
        out_shape=jax.ShapeDtypeStruct((GROUP, HD + STATS, ROWS), jnp.bfloat16),
        in_specs=[smem, smem, vmem, vmem] + [pl.BlockSpec(memory_space=pl.ANY)] * NY,
        out_specs=vmem,
        scratch_shapes=[
            pltpu.VMEM((NY * SLOTS, 2, BLOCK, HD), jnp.bfloat16),
            pltpu.VMEM((1, ROWS), jnp.float32),
            pltpu.VMEM((1, ROWS), jnp.float32),
            pltpu.VMEM((HD, ROWS), jnp.float32),
            pltpu.SemaphoreType.DMA((NY,)),
        ],
        compiler_params=pltpu.CompilerParams(vmem_limit_bytes=32 << 20),
        name="attend",
    )(lists, own, queries, new_kv, *shards)


def project_kernel(parts, weight, out, attended):
    @pl.when(pl.program_id(0) == 0)
    def _():
        levels = []
        for i in range(GROUP):
            stats = parts[i, pl.ds(HD, STATS), :].astype(jnp.float32)
            levels.append(stats[0:1] + stats[1:2] + stats[2:3])
        top = levels[0]
        for level in levels[1:]:
            top = jnp.maximum(top, level)
        shares = [jnp.exp2(level - top) for level in levels]
        whole = shares[0]
        for share in shares[1:]:
            whole = whole + share
        for h in range(PER):
            columns = pl.ds(h * TOK, TOK)
            mixed = jnp.zeros((HD, TOK), jnp.float32)
            for i in range(GROUP):
                mixed = mixed + parts[i, pl.ds(0, HD), columns].astype(jnp.float32) * (shares[i] / whole)[:, h * TOK:(h + 1) * TOK]
            attended[:, h * HD:(h + 1) * HD] = jnp.transpose(mixed).astype(jnp.bfloat16)

    out[...] = jnp.dot(attended[...], weight[...], preferred_element_type=jnp.float32).astype(jnp.bfloat16)


def project(parts, weight):
    width = weight.shape[1]
    step = 1024
    return pl.pallas_call(
        project_kernel,
        out_shape=jax.ShapeDtypeStruct((TOK, width), jnp.bfloat16),
        grid=(width // step,),
        in_specs=[
            pl.BlockSpec((GROUP, HD + STATS, ROWS), lambda n: (0, 0, 0)),
            pl.BlockSpec((ROWS, step), lambda n: (0, n)),
        ],
        out_specs=pl.BlockSpec((TOK, step), lambda n: (0, n)),
        scratch_shapes=[pltpu.VMEM((TOK, ROWS), jnp.bfloat16)],
        compiler_params=pltpu.CompilerParams(vmem_limit_bytes=32 << 20),
        name="project",
    )(parts, weight)


def block_lists(block_owner, block_slot, prefix_blocks, x, y, c):
    pick = lambda a: lax.dynamic_index_in_dim(a.reshape(NX, NY, NC, -1), y, 1, keepdims=False).reshape(GROUP, -1)
    owners, slots, lengths = pick(block_owner), pick(block_slot), pick(prefix_blocks)
    column = owners // (NY * NC) * NC + owners % NC
    ring = (owners // NC - y) % NY
    places = jnp.arange(MAXB, dtype=jnp.int32)
    mine = (column == x * NC + c) & (places[None, :] < lengths)
    earlier = (places[:, None] <= places[None, :]).astype(jnp.float32)
    ranks = jnp.dot(mine.astype(jnp.float32), earlier).astype(jnp.int32) - 1
    codes = ring * SLOTS + slots
    matches = mine[:, None, :] & (ranks[:, None, :] == jnp.arange(LIST, dtype=jnp.int32)[None, :, None])
    lists = jnp.sum(jnp.where(matches, codes[:, None, :], 0), axis=2)
    counts = jnp.sum(mine.astype(jnp.int32), axis=1, keepdims=True)
    return jnp.concatenate([lists, counts], axis=1)


def local(queries, new_kv, cache, block_owner, block_slot, prefix_blocks, out_weight):
    x, y, c = lax.axis_index("x"), lax.axis_index("y"), lax.axis_index("c")
    gathered = lax.all_gather(queries, ("x", "c"), axis=0)
    up = [(i, (i + 1) % NY) for i in range(NY)]
    down = [(i, (i - 1) % NY) for i in range(NY)]
    shards = [cache] * NY
    below = above = cache
    for step in range(1, NY // 2 + 1):
        below = lax.ppermute(below, "y", up)
        shards[NY - step] = below
        if step < NY // 2:
            above = lax.ppermute(above, "y", down)
            shards[step] = above
    lists = block_lists(block_owner, block_slot, prefix_blocks, x, y, c)
    own = (x * NC + c).reshape(1)
    parts = attend(lists, own, gathered, new_kv, shards)
    parts = lax.all_to_all(parts, ("x", "c"), split_axis=0, concat_axis=0, tiled=True)
    partial = project(parts, out_weight).reshape(NZ, TOK // NZ, -1)
    arrived = lax.all_to_all(partial, "z", split_axis=0, concat_axis=0, tiled=True)
    return jnp.sum(arrived.astype(jnp.float32), axis=0).astype(jnp.bfloat16)


def solution(mesh):
    fine = Mesh(mesh.devices.reshape(NX, NY, NC, NZ), ("x", "y", "c", "z"))
    replica = ("x", "y", "c")
    placed = (
        P(replica, "z"),
        P(None, replica, "z"),
        P(replica, None, None, "z"),
        P(),
        P(),
        P(),
        P("z", None),
    )
    return jax.shard_map(
        local, mesh=fine, in_specs=placed, out_specs=P(("x", "y", "c", "z"), None), check_vma=False
    )
```

```python
import math

import jax
import jax.numpy as jnp
from jax import lax
from jax.experimental import pallas as pl
from jax.experimental.pallas import tpu as pltpu
from jax.sharding import Mesh, PartitionSpec as P

HQ = 32
KVH = 8
HD = 128
BLOCK = 64
MAXB = 64
NX, NY, NC, NZ = 4, 8, 2, 8
GROUP = NX * NC
PER = HQ // KVH
TOK = 128
ROWS = PER * TOK
SLOTS = 8
CAP = 2
LIST = NY * CAP
TILE = 4
PAIR = 2
STATS = 16
NEGATIVE = -1e30
FLOOR = -1e29
LOG2 = HD ** (-0.5) * math.log2(math.e)


def contract(a, b, da, db):
    return lax.dot_general(a, b, (((da,), (db,)), ((), ())), preferred_element_type=jnp.float32)


def lists_kernel(x, y, c, lengths, owners, slots, lists):
    rows = [(g // NC * NY + y[0]) * NC + g % NC for g in range(GROUP)]
    owner = jnp.concatenate([owners[pl.ds(r, 1), :] for r in rows], axis=0)
    slot = jnp.concatenate([slots[pl.ds(r, 1), :] for r in rows], axis=0)
    length = jnp.concatenate([jnp.full((1, MAXB), lengths[r], jnp.int32) for r in rows], axis=0)
    place = lax.broadcasted_iota(jnp.int32, (GROUP, MAXB), 1)
    mine = (owner // (NY * NC) == x[0]) & (owner % NC == c[0]) & (place < length)
    code = ((owner // NC - y[0]) * (1 - 2 * c[0]) + 2 * NY) % NY * SLOTS + slot
    earlier = lax.broadcasted_iota(jnp.int32, (MAXB, MAXB), 0) < lax.broadcasted_iota(jnp.int32, (MAXB, MAXB), 1)
    flags = mine.astype(jnp.float32)
    ranks = jnp.dot(flags, earlier.astype(jnp.float32), preferred_element_type=jnp.float32)
    lane = lax.broadcasted_iota(jnp.int32, (GROUP, HD), 1)
    table = jnp.where(lane == LIST, jnp.sum(flags, axis=1, keepdims=True), 0.0)
    code = jnp.where(mine, code.astype(jnp.float32), 0.0)
    for k in range(LIST):
        entry = jnp.sum(jnp.where(ranks == k, code, 0.0), axis=1, keepdims=True)
        table = jnp.where(lane == k, entry, table)
    lists[...] = table.astype(jnp.int32)


def block_lists(x, y, c, lengths, owners, slots):
    vmem, smem = pl.BlockSpec(memory_space=pltpu.VMEM), pl.BlockSpec(memory_space=pltpu.SMEM)
    return pl.pallas_call(
        lists_kernel,
        out_shape=pltpu.VMEM((GROUP, HD), jnp.int32),
        in_specs=[smem] * 4 + [vmem] * 2,
        out_specs=vmem,
        compiler_params=pltpu.CompilerParams(vmem_limit_bytes=4 << 20),
        name="block_lists",
    )(x, y, c, lengths, *(pltpu.with_memory_space_constraint(a, pltpu.HBM) for a in (owners, slots)))


def attend_kernel(x, c, lists, new_kv, *rest):
    shards, asked, rest = rest[:NY], rest[NY:NY + NC], rest[NY + NC:]
    out, queries, fresh, held, peak, total, weighted, sems = rest
    first = [pltpu.make_async_copy(asked[d], queries.at[d], sems.at[NY + d]) for d in range(NC)]
    first.append(pltpu.make_async_copy(new_kv, fresh, sems.at[NY + NC]))
    later = [pltpu.make_async_copy(shards[s], held.at[pl.ds(s * SLOTS, SLOTS)], sems.at[s]) for s in range(NY)]
    for copy in first + later:
        copy.start()
    own = x[0] * NC + c[0]

    def heads(g):
        q = queries[(g + c[0]) % NC, g // NC]
        return jnp.concatenate([q[:, h * HD:(h + 1) * HD] for h in range(PER)], axis=0)

    def fold(p, scores, values):
        top = jnp.maximum(peak[p], jnp.max(scores, axis=0, keepdims=True))
        factor = jnp.exp2((peak[p] - top) * LOG2)
        weights = jnp.exp2((scores - top) * LOG2)
        peak[p] = top
        total[p] = total[p] * factor + jnp.sum(weights, axis=0, keepdims=True)
        weighted[p] = weighted[p] * factor + contract(values, weights.astype(jnp.bfloat16), 0, 0)

    def reset(p):
        peak[p] = jnp.full((1, ROWS), FLOOR, jnp.float32)
        total[p] = jnp.zeros((1, ROWS), jnp.float32)
        weighted[p] = jnp.zeros((HD, ROWS), jnp.float32)

    reset(0)
    for copy in first:
        copy.wait()
    scores = contract(fresh[0], heads(own), 1, 1)
    key = lax.broadcasted_iota(jnp.int32, (TOK, ROWS), 0)
    token = lax.broadcasted_iota(jnp.int32, (TOK, ROWS), 1) % TOK
    fold(0, jnp.where(key <= token, scores, NEGATIVE), fresh[1])
    for copy in later:
        copy.wait()

    def finish(p, g):
        filled = total[p] > 0.0
        safe = jnp.where(filled, total[p], 1.0)
        level = jnp.where(filled, peak[p] * LOG2 + jnp.log2(safe), NEGATIVE)
        high = level.astype(jnp.bfloat16).astype(jnp.float32)
        middle = (level - high).astype(jnp.bfloat16).astype(jnp.float32)
        row = lax.broadcasted_iota(jnp.int32, (STATS, ROWS), 0)
        stats = jnp.where(row == 0, high, jnp.where(row == 1, middle, jnp.where(row == 2, level - high - middle, 0.0)))
        out[g, pl.ds(0, HD), :] = (weighted[p] * (1.0 / safe)).astype(jnp.bfloat16)
        out[g, pl.ds(HD, STATS), :] = stats.astype(jnp.bfloat16)

    def one_pair(i, carry):
        pair = [(own + i * PAIR + p) % GROUP for p in range(PAIR)]
        counts = [lists[g, LIST] for g in pair]
        for p in range(PAIR):
            if p:
                reset(p)
            else:
                pl.when(i > 0)(lambda: reset(0))

        def one_tile(j, carry):
            loaded = []
            for g, count in zip(pair, counts):
                ids = [lists[g, j * TILE + k] for k in range(TILE)]
                keys = jnp.concatenate([held[b, 0] for b in ids], axis=0)
                values = jnp.concatenate([held[b, 1] for b in ids], axis=0)
                scores = contract(keys, heads(g), 1, 1)
                place = lax.broadcasted_iota(jnp.int32, scores.shape, 0)
                loaded.append((jnp.where(place < (count - j * TILE) * BLOCK, scores, NEGATIVE), values))
            for p, (scores, values) in enumerate(loaded):
                fold(p, scores, values)
            return carry

        longest = counts[0]
        for count in counts[1:]:
            longest = jnp.maximum(longest, count)
        lax.fori_loop(0, (longest + TILE - 1) // TILE, one_tile, 0)
        for p, g in enumerate(pair):
            finish(p, g)
        return carry

    lax.fori_loop(0, GROUP // PAIR, one_pair, 0)


def attend(x, c, lists, new_kv, asked, shards):
    vmem, smem, free = (pl.BlockSpec(memory_space=m) for m in (pltpu.VMEM, pltpu.SMEM, pl.ANY))
    new_kv, own = (pltpu.with_memory_space_constraint(a, pltpu.HBM) for a in (new_kv, shards[0]))
    return pl.pallas_call(
        attend_kernel,
        out_shape=jax.ShapeDtypeStruct((GROUP, HD + STATS, ROWS), jnp.bfloat16),
        in_specs=[smem, smem, smem] + [free] * (1 + NC + NY),
        out_specs=vmem,
        scratch_shapes=[
            pltpu.VMEM((NC, NX, TOK, ROWS), jnp.bfloat16),
            pltpu.VMEM((2, TOK, HD), jnp.bfloat16),
            pltpu.VMEM((NY * SLOTS, 2, BLOCK, HD), jnp.bfloat16),
            pltpu.VMEM((PAIR, 1, ROWS), jnp.float32),
            pltpu.VMEM((PAIR, 1, ROWS), jnp.float32),
            pltpu.VMEM((PAIR, HD, ROWS), jnp.float32),
            pltpu.SemaphoreType.DMA((NY + NC + 1,)),
        ],
        compiler_params=pltpu.CompilerParams(vmem_limit_bytes=16 << 20),
        name="attend",
    )(x, c, lists, new_kv, own, *shards[1:], *asked)


def project_kernel(parts, weight, out, attended):
    @pl.when(pl.program_id(0) == 0)
    def _():
        levels = []
        for i in range(GROUP):
            stats = parts[i, pl.ds(HD, STATS), :].astype(jnp.float32)
            levels.append(stats[0:1] + stats[1:2] + stats[2:3])
        top = levels[0]
        for level in levels[1:]:
            top = jnp.maximum(top, level)
        shares = [jnp.exp2(level - top) for level in levels]
        whole = shares[0]
        for share in shares[1:]:
            whole = whole + share
        for h in range(PER):
            columns = pl.ds(h * TOK, TOK)
            mixed = jnp.zeros((HD, TOK), jnp.float32)
            for i in range(GROUP):
                mixed = mixed + parts[i, pl.ds(0, HD), columns].astype(jnp.float32) * (shares[i] / whole)[:, h * TOK:(h + 1) * TOK]
            attended[:, h * HD:(h + 1) * HD] = jnp.transpose(mixed).astype(jnp.bfloat16)

    out[...] = jnp.dot(attended[...], weight[...], preferred_element_type=jnp.float32).astype(jnp.bfloat16)


def project(parts, weight):
    width = weight.shape[1]
    step = 1024
    return pl.pallas_call(
        project_kernel,
        out_shape=jax.ShapeDtypeStruct((TOK, width), jnp.bfloat16),
        grid=(width // step,),
        in_specs=[
            pl.BlockSpec((GROUP, HD + STATS, ROWS), lambda n: (0, 0, 0)),
            pl.BlockSpec((ROWS, step), lambda n: (0, n)),
        ],
        out_specs=pl.BlockSpec((TOK, step), lambda n: (0, n)),
        scratch_shapes=[pltpu.VMEM((TOK, ROWS), jnp.bfloat16)],
        compiler_params=pltpu.CompilerParams(vmem_limit_bytes=16 << 20),
        name="project",
    )(parts, weight)


def spread(cache, queries):
    def shift(a, hops):
        pairs = [(y * NC + c, (y + hops * (1 - 2 * c)) % NY * NC + c) for y in range(NY) for c in range(NC)]
        return lax.ppermute(a, ("y", "c"), pairs)

    behind2, ahead2 = shift(cache, 2), shift(cache, -2)
    behind1, ahead1 = shift(cache, 1), shift(cache, -1)
    across, behind3, ahead3 = shift(behind2, 2), shift(behind2, 1), shift(ahead2, -1)
    same = lax.all_gather(queries, "x", axis=0)
    later = (behind1, ahead1, across, behind3, ahead3)
    same, behind1, ahead1, across, behind3, ahead3 = lax.optimization_barrier((same, *later))
    swapped = lax.ppermute(same, "c", [(0, 1), (1, 0)])
    return [cache, ahead1, ahead2, ahead3, across, behind3, behind2, behind1], [same, swapped]


def local(queries, new_kv, cache, block_owner, block_slot, prefix_blocks, out_weight):
    x, y, c = (lax.axis_index(name).reshape(1) for name in ("x", "y", "c"))
    shards, asked = spread(cache, queries)
    lists = block_lists(x, y, c, prefix_blocks, block_owner, block_slot)
    parts = attend(x, c, lists, new_kv, asked, shards)
    parts = lax.all_to_all(parts, ("x", "c"), split_axis=0, concat_axis=0, tiled=True)
    partial = project(parts, out_weight).reshape(NZ, TOK // NZ, -1)
    arrived = lax.all_to_all(partial, "z", split_axis=0, concat_axis=0, tiled=True)
    return jnp.sum(arrived.astype(jnp.float32), axis=0).astype(jnp.bfloat16)


def solution(mesh):
    fine = Mesh(mesh.devices.reshape(NX, NY, NC, NZ), ("x", "y", "c", "z"))
    replica = ("x", "y", "c")
    placed = (
        P(replica, "z"),
        P(None, replica, "z"),
        P(replica, None, None, "z"),
        P(),
        P(),
        P(),
        P("z", None),
    )
    return jax.shard_map(
        local, mesh=fine, in_specs=placed, out_specs=P(("x", "y", "c", "z"), None), check_vma=False
    )
```

```python
import math

import jax
import jax.numpy as jnp
from jax import lax
from jax.experimental import pallas as pl
from jax.experimental.pallas import tpu as pltpu
from jax.sharding import Mesh, PartitionSpec as P

HQ = 32
KVH = 8
HD = 128
BLOCK = 64
MAXB = 64
NX, NY, NC, NZ = 4, 8, 2, 8
GROUP = NX * NC
PER = HQ // KVH
TOK = 128
ROWS = PER * TOK
SLOTS = 8
CAP = 2
LIST = NY * CAP
TILE = 4
PAIR = 4
STATS = 16
NEGATIVE = -1e30
FLOOR = -1e29
LOG2 = HD ** (-0.5) * math.log2(math.e)


def contract(a, b, da, db):
    return lax.dot_general(a, b, (((da,), (db,)), ((), ())), preferred_element_type=jnp.float32)


def lists_kernel(x, y, c, lengths, owners, slots, lists):
    rows = [(g // NC * NY + y[0]) * NC + g % NC for g in range(GROUP)]
    owner = jnp.concatenate([owners[pl.ds(r, 1), :] for r in rows], axis=0)
    slot = jnp.concatenate([slots[pl.ds(r, 1), :] for r in rows], axis=0)
    length = jnp.concatenate([jnp.full((1, MAXB), lengths[r], jnp.int32) for r in rows], axis=0)
    place = lax.broadcasted_iota(jnp.int32, (GROUP, MAXB), 1)
    mine = (owner // (NY * NC) == x[0]) & (owner % NC == c[0]) & (place < length)
    code = ((owner // NC - y[0]) * (1 - 2 * c[0]) + 2 * NY) % NY * SLOTS + slot
    earlier = lax.broadcasted_iota(jnp.int32, (MAXB, MAXB), 0) < lax.broadcasted_iota(jnp.int32, (MAXB, MAXB), 1)
    flags = mine.astype(jnp.float32)
    ranks = jnp.dot(flags, earlier.astype(jnp.float32), preferred_element_type=jnp.float32)
    lane = lax.broadcasted_iota(jnp.int32, (GROUP, HD), 1)
    table = jnp.where(lane == LIST, jnp.sum(flags, axis=1, keepdims=True), 0.0)
    code = jnp.where(mine, code.astype(jnp.float32), 0.0)
    for k in range(LIST):
        entry = jnp.sum(jnp.where(ranks == k, code, 0.0), axis=1, keepdims=True)
        table = jnp.where(lane == k, entry, table)
    lists[...] = table.astype(jnp.int32)


def block_lists(x, y, c, lengths, owners, slots):
    vmem, smem = pl.BlockSpec(memory_space=pltpu.VMEM), pl.BlockSpec(memory_space=pltpu.SMEM)
    return pl.pallas_call(
        lists_kernel,
        out_shape=pltpu.VMEM((GROUP, HD), jnp.int32),
        in_specs=[smem] * 4 + [vmem] * 2,
        out_specs=vmem,
        compiler_params=pltpu.CompilerParams(vmem_limit_bytes=4 << 20),
        name="block_lists",
    )(x, y, c, lengths, *(pltpu.with_memory_space_constraint(a, pltpu.HBM) for a in (owners, slots)))


def attend_kernel(x, c, lists, new_kv, *rest):
    shards, asked, rest = rest[:NY], rest[NY:NY + NC], rest[NY + NC:]
    out, queries, fresh, held, peak, total, weighted, order, sems = rest
    first = [pltpu.make_async_copy(asked[d], queries.at[d], sems.at[NY + d]) for d in range(NC)]
    first.append(pltpu.make_async_copy(new_kv, fresh, sems.at[NY + NC]))
    later = [pltpu.make_async_copy(shards[s], held.at[pl.ds(s * SLOTS, SLOTS)], sems.at[s]) for s in range(NY)]
    for copy in first + later:
        copy.start()
    own = x[0] * NC + c[0]

    def heads(g):
        q = queries[(g + c[0]) % NC, g // NC]
        return jnp.concatenate([q[:, h * HD:(h + 1) * HD] for h in range(PER)], axis=0)

    def reduce(scores, values):
        top = jnp.maximum(jnp.max(scores, axis=0, keepdims=True), FLOOR)
        weights = jnp.exp2((scores - top) * LOG2)
        return top, jnp.sum(weights, axis=0, keepdims=True), contract(values, weights.astype(jnp.bfloat16), 0, 0)

    def merge(g, top, amount, product):
        highest = jnp.maximum(peak[g], top)
        before, now = jnp.exp2((peak[g] - highest) * LOG2), jnp.exp2((top - highest) * LOG2)
        peak[g] = highest
        total[g] = total[g] * before + amount * now
        weighted[g] = weighted[g] * before + product * now

    def append(entry, used):
        g, j = entry % GROUP, entry // GROUP
        wanted = lists[g, LIST] > j * TILE

        @pl.when(wanted)
        def _():
            order[used] = entry

        return used + wanted.astype(jnp.int32)

    peak[...] = jnp.full(peak.shape, FLOOR, jnp.float32)
    total[...] = jnp.zeros(total.shape, jnp.float32)
    weighted[...] = jnp.zeros(weighted.shape, jnp.float32)
    used = lax.fori_loop(0, GROUP * LIST // TILE, append, 0)
    for p in range(PAIR):
        order[used + p] = GROUP * LIST // TILE

    for copy in first:
        copy.wait()
    scores = contract(fresh[0], heads(own), 1, 1)
    key = lax.broadcasted_iota(jnp.int32, (TOK, ROWS), 0)
    token = lax.broadcasted_iota(jnp.int32, (TOK, ROWS), 1) % TOK
    merge(own, *reduce(jnp.where(key <= token, scores, NEGATIVE), fresh[1]))
    for copy in later:
        copy.wait()

    def some_tiles(i, carry):
        results = []
        for p in range(PAIR):
            entry = order[i * PAIR + p]
            valid = entry < GROUP * LIST // TILE
            g, j = entry % GROUP, jnp.where(valid, entry // GROUP, 0)
            left = jnp.where(valid, (lists[g, LIST] - j * TILE) * BLOCK, 0)
            ids = [lists[g, j * TILE + k] for k in range(TILE)]
            keys = jnp.concatenate([held[b, 0] for b in ids], axis=0)
            values = jnp.concatenate([held[b, 1] for b in ids], axis=0)
            scores = contract(keys, heads(g), 1, 1)
            place = lax.broadcasted_iota(jnp.int32, scores.shape, 0)
            results.append((g, *reduce(jnp.where(place < left, scores, NEGATIVE), values)))
        for result in results:
            merge(*result)
        return carry

    lax.fori_loop(0, (used + PAIR - 1) // PAIR, some_tiles, 0)

    def finish(g, carry):
        filled = total[g] > 0.0
        safe = jnp.where(filled, total[g], 1.0)
        level = jnp.where(filled, peak[g] * LOG2 + jnp.log2(safe), NEGATIVE)
        high = level.astype(jnp.bfloat16).astype(jnp.float32)
        middle = (level - high).astype(jnp.bfloat16).astype(jnp.float32)
        row = lax.broadcasted_iota(jnp.int32, (STATS, ROWS), 0)
        stats = jnp.where(row == 0, high, jnp.where(row == 1, middle, jnp.where(row == 2, level - high - middle, 0.0)))
        out[g, pl.ds(0, HD), :] = (weighted[g] * (1.0 / safe)).astype(jnp.bfloat16)
        out[g, pl.ds(HD, STATS), :] = stats.astype(jnp.bfloat16)
        return carry

    lax.fori_loop(0, GROUP, finish, 0)


def attend(x, c, lists, new_kv, asked, shards):
    vmem, smem, free = (pl.BlockSpec(memory_space=m) for m in (pltpu.VMEM, pltpu.SMEM, pl.ANY))
    new_kv, own = (pltpu.with_memory_space_constraint(a, pltpu.HBM) for a in (new_kv, shards[0]))
    return pl.pallas_call(
        attend_kernel,
        out_shape=jax.ShapeDtypeStruct((GROUP, HD + STATS, ROWS), jnp.bfloat16),
        in_specs=[smem, smem, smem] + [free] * (1 + NC + NY),
        out_specs=vmem,
        scratch_shapes=[
            pltpu.VMEM((NC, NX, TOK, ROWS), jnp.bfloat16),
            pltpu.VMEM((2, TOK, HD), jnp.bfloat16),
            pltpu.VMEM((NY * SLOTS, 2, BLOCK, HD), jnp.bfloat16),
            pltpu.VMEM((GROUP, 1, ROWS), jnp.float32),
            pltpu.VMEM((GROUP, 1, ROWS), jnp.float32),
            pltpu.VMEM((GROUP, HD, ROWS), jnp.float32),
            pltpu.SMEM((GROUP * LIST // TILE + PAIR,), jnp.int32),
            pltpu.SemaphoreType.DMA((NY + NC + 1,)),
        ],
        compiler_params=pltpu.CompilerParams(vmem_limit_bytes=16 << 20),
        name="attend",
    )(x, c, lists, new_kv, own, *shards[1:], *asked)


def project_kernel(parts, weight, out, attended):
    @pl.when(pl.program_id(0) == 0)
    def _():
        levels = []
        for i in range(GROUP):
            stats = parts[i, pl.ds(HD, STATS), :].astype(jnp.float32)
            levels.append(stats[0:1] + stats[1:2] + stats[2:3])
        top = levels[0]
        for level in levels[1:]:
            top = jnp.maximum(top, level)
        shares = [jnp.exp2(level - top) for level in levels]
        whole = shares[0]
        for share in shares[1:]:
            whole = whole + share
        for h in range(PER):
            columns = pl.ds(h * TOK, TOK)
            mixed = jnp.zeros((HD, TOK), jnp.float32)
            for i in range(GROUP):
                mixed = mixed + parts[i, pl.ds(0, HD), columns].astype(jnp.float32) * (shares[i] / whole)[:, h * TOK:(h + 1) * TOK]
            attended[:, h * HD:(h + 1) * HD] = jnp.transpose(mixed).astype(jnp.bfloat16)

    out[...] = jnp.dot(attended[...], weight[...], preferred_element_type=jnp.float32).astype(jnp.bfloat16)


def project(parts, weight):
    width = weight.shape[1]
    step = 1024
    return pl.pallas_call(
        project_kernel,
        out_shape=jax.ShapeDtypeStruct((TOK, width), jnp.bfloat16),
        grid=(width // step,),
        in_specs=[
            pl.BlockSpec((GROUP, HD + STATS, ROWS), lambda n: (0, 0, 0)),
            pl.BlockSpec((ROWS, step), lambda n: (0, n)),
        ],
        out_specs=pl.BlockSpec((TOK, step), lambda n: (0, n)),
        scratch_shapes=[pltpu.VMEM((TOK, ROWS), jnp.bfloat16)],
        compiler_params=pltpu.CompilerParams(vmem_limit_bytes=16 << 20),
        name="project",
    )(parts, weight)


def spread(cache, queries):
    def shift(a, hops):
        pairs = [(y * NC + c, (y + hops * (1 - 2 * c)) % NY * NC + c) for y in range(NY) for c in range(NC)]
        return lax.ppermute(a, ("y", "c"), pairs)

    behind2, ahead2 = shift(cache, 2), shift(cache, -2)
    behind1, ahead1 = shift(cache, 1), shift(cache, -1)
    across, behind3, ahead3 = shift(behind2, 2), shift(behind2, 1), shift(ahead2, -1)
    same = lax.all_gather(queries, "x", axis=0)
    later = (behind1, ahead1, across, behind3, ahead3)
    same, behind1, ahead1, across, behind3, ahead3 = lax.optimization_barrier((same, *later))
    swapped = lax.ppermute(same, "c", [(0, 1), (1, 0)])
    return [cache, ahead1, ahead2, ahead3, across, behind3, behind2, behind1], [same, swapped]


def local(queries, new_kv, cache, block_owner, block_slot, prefix_blocks, out_weight):
    x, y, c = (lax.axis_index(name).reshape(1) for name in ("x", "y", "c"))
    shards, asked = spread(cache, queries)
    lists = block_lists(x, y, c, prefix_blocks, block_owner, block_slot)
    parts = attend(x, c, lists, new_kv, asked, shards)
    parts = lax.all_to_all(parts, ("x", "c"), split_axis=0, concat_axis=0, tiled=True)
    partial = project(parts, out_weight).reshape(NZ, TOK // NZ, -1)
    arrived = lax.all_to_all(partial, "z", split_axis=0, concat_axis=0, tiled=True)
    return jnp.sum(arrived.astype(jnp.float32), axis=0).astype(jnp.bfloat16)


def solution(mesh):
    fine = Mesh(mesh.devices.reshape(NX, NY, NC, NZ), ("x", "y", "c", "z"))
    replica = ("x", "y", "c")
    placed = (
        P(replica, "z"),
        P(None, replica, "z"),
        P(replica, None, None, "z"),
        P(),
        P(),
        P(),
        P("z", None),
    )
    return jax.shard_map(
        local, mesh=fine, in_specs=placed, out_specs=P(("x", "y", "c", "z"), None), check_vma=False
    )
```

```python
import functools
import math

import jax
import jax.numpy as jnp
from jax import lax
from jax.experimental import pallas as pl
from jax.experimental.pallas import tpu as pltpu
from jax.sharding import Mesh, PartitionSpec as P

HQ = 32
KVH = 8
HD = 128
BLOCK = 64
MAXB = 64
NX, NY, NC, NZ = 4, 8, 2, 8
GROUP = NX * NC
PER = HQ // KVH
TOK = 128
ROWS = PER * TOK
SLOTS = 8
CAP = 2
LIST = NY * CAP
TILE = 4
ENTRIES = NX * LIST // TILE
PAIR = 4
STATS = 16
NEGATIVE = -1e30
FLOOR = -1e29
LOG2 = HD ** (-0.5) * math.log2(math.e)


def contract(a, b, da, db):
    return lax.dot_general(a, b, (((da,), (db,)), ((), ())), preferred_element_type=jnp.float32)


def lists_kernel(x, y, c, lengths, owners, slots, lists):
    rows = [(g // NC * NY + y[0]) * NC + g % NC for g in range(GROUP)]
    owner = jnp.concatenate([owners[pl.ds(r, 1), :] for r in rows], axis=0)
    slot = jnp.concatenate([slots[pl.ds(r, 1), :] for r in rows], axis=0)
    length = jnp.concatenate([jnp.full((1, MAXB), lengths[r], jnp.int32) for r in rows], axis=0)
    place = lax.broadcasted_iota(jnp.int32, (GROUP, MAXB), 1)
    mine = (owner // (NY * NC) == x[0]) & (owner % NC == c[0]) & (place < length)
    code = ((owner // NC - y[0]) * (1 - 2 * c[0]) + 2 * NY) % NY * SLOTS + slot
    earlier = lax.broadcasted_iota(jnp.int32, (MAXB, MAXB), 0) < lax.broadcasted_iota(jnp.int32, (MAXB, MAXB), 1)
    flags = mine.astype(jnp.float32)
    ranks = jnp.dot(flags, earlier.astype(jnp.float32), preferred_element_type=jnp.float32)
    lane = lax.broadcasted_iota(jnp.int32, (GROUP, HD), 1)
    table = jnp.where(lane == LIST, jnp.sum(flags, axis=1, keepdims=True), 0.0)
    code = jnp.where(mine, code.astype(jnp.float32), 0.0)
    for k in range(LIST):
        entry = jnp.sum(jnp.where(ranks == k, code, 0.0), axis=1, keepdims=True)
        table = jnp.where(lane == k, entry, table)
    lists[...] = table.astype(jnp.int32)


def block_lists(x, y, c, lengths, owners, slots):
    vmem, smem = pl.BlockSpec(memory_space=pltpu.VMEM), pl.BlockSpec(memory_space=pltpu.SMEM)
    return pl.pallas_call(
        lists_kernel,
        out_shape=pltpu.VMEM((GROUP, HD), jnp.int32),
        in_specs=[smem] * 4 + [vmem] * 2,
        out_specs=vmem,
        compiler_params=pltpu.CompilerParams(vmem_limit_bytes=4 << 20),
        name="block_lists",
    )(x, y, c, lengths, *(pltpu.with_memory_space_constraint(a, pltpu.HBM) for a in (owners, slots)))


def split_level(level):
    high = level.astype(jnp.bfloat16).astype(jnp.float32)
    middle = (level - high).astype(jnp.bfloat16).astype(jnp.float32)
    row = lax.broadcasted_iota(jnp.int32, (STATS, ROWS), 0)
    stats = jnp.where(row == 0, high, jnp.where(row == 1, middle, jnp.where(row == 2, level - high - middle, 0.0)))
    return stats.astype(jnp.bfloat16)


def join_level(stats):
    stats = stats.astype(jnp.float32)
    return stats[0:1] + stats[1:2] + stats[2:3]


def attend_kernel(home, x, core, lists, new_kv, *rest):
    shards, asked, rest = rest[:NY], rest[NY], rest[NY + 1:]
    out, queries, fresh, held, peak, total, weighted, order, sems = rest
    first = [pltpu.make_async_copy(asked, queries, sems.at[NY])]
    if home:
        first.append(pltpu.make_async_copy(new_kv, fresh, sems.at[NY + 1]))
    later = [pltpu.make_async_copy(shards[s], held.at[pl.ds(s * SLOTS, SLOTS)], sems.at[s]) for s in range(NY)]
    for copy in first + later:
        copy.start()
    def heads(g):
        q = queries[g]
        return jnp.concatenate([q[:, h * HD:(h + 1) * HD] for h in range(PER)], axis=0)

    def reduce(scores, values):
        top = jnp.maximum(jnp.max(scores, axis=0, keepdims=True), FLOOR)
        weights = jnp.exp2((scores - top) * LOG2)
        return top, jnp.sum(weights, axis=0, keepdims=True), contract(values, weights.astype(jnp.bfloat16), 0, 0)

    def merge(g, top, amount, product):
        highest = jnp.maximum(peak[g], top)
        before, now = jnp.exp2((peak[g] - highest) * LOG2), jnp.exp2((top - highest) * LOG2)
        peak[g] = highest
        total[g] = total[g] * before + amount * now
        weighted[g] = weighted[g] * before + product * now

    def append(entry, used):
        g, j = entry % NX, entry // NX
        wanted = lists[g * NC + core[0], LIST] > j * TILE

        @pl.when(wanted)
        def _():
            order[used] = entry

        return used + wanted.astype(jnp.int32)

    peak[...] = jnp.full(peak.shape, FLOOR, jnp.float32)
    total[...] = jnp.zeros(total.shape, jnp.float32)
    weighted[...] = jnp.zeros(weighted.shape, jnp.float32)
    used = lax.fori_loop(0, ENTRIES, append, 0)
    for p in range(PAIR):
        order[used + p] = ENTRIES

    for copy in first:
        copy.wait()
    if home:
        scores = contract(fresh[0], heads(x[0]), 1, 1)
        key = lax.broadcasted_iota(jnp.int32, (TOK, ROWS), 0)
        token = lax.broadcasted_iota(jnp.int32, (TOK, ROWS), 1) % TOK
        merge(x[0], *reduce(jnp.where(key <= token, scores, NEGATIVE), fresh[1]))
    for copy in later:
        copy.wait()

    def some_tiles(i, carry):
        results = []
        for p in range(PAIR):
            entry = order[i * PAIR + p]
            valid = entry < ENTRIES
            g, j = entry % NX, jnp.where(valid, entry // NX, 0)
            row = g * NC + core[0]
            left = jnp.where(valid, (lists[row, LIST] - j * TILE) * BLOCK, 0)
            ids = [lists[row, j * TILE + k] for k in range(TILE)]
            keys = jnp.concatenate([held[b, 0] for b in ids], axis=0)
            values = jnp.concatenate([held[b, 1] for b in ids], axis=0)
            scores = contract(keys, heads(g), 1, 1)
            place = lax.broadcasted_iota(jnp.int32, scores.shape, 0)
            results.append((g, *reduce(jnp.where(place < left, scores, NEGATIVE), values)))
        for result in results:
            merge(*result)
        return carry

    lax.fori_loop(0, (used + PAIR - 1) // PAIR, some_tiles, 0)

    def finish(g, carry):
        filled = total[g] > 0.0
        safe = jnp.where(filled, total[g], 1.0)
        level = jnp.where(filled, peak[g] * LOG2 + jnp.log2(safe), NEGATIVE)
        out[g, pl.ds(0, HD), :] = (weighted[g] * (1.0 / safe)).astype(jnp.bfloat16)
        out[g, pl.ds(HD, STATS), :] = split_level(level)
        return carry

    lax.fori_loop(0, NX, finish, 0)


def attend(home, x, core, lists, new_kv, asked, shards):
    vmem, smem, free = (pl.BlockSpec(memory_space=m) for m in (pltpu.VMEM, pltpu.SMEM, pl.ANY))
    new_kv, own = (pltpu.with_memory_space_constraint(a, pltpu.HBM) for a in (new_kv, shards[0]))
    return pl.pallas_call(
        functools.partial(attend_kernel, home),
        out_shape=jax.ShapeDtypeStruct((NX, HD + STATS, ROWS), jnp.bfloat16),
        in_specs=[smem, smem, smem] + [free] * (2 + NY),
        out_specs=vmem,
        scratch_shapes=[
            pltpu.VMEM((NX, TOK, ROWS), jnp.bfloat16),
            pltpu.VMEM((2, TOK, HD), jnp.bfloat16),
            pltpu.VMEM((NY * SLOTS, 2, BLOCK, HD), jnp.bfloat16),
            pltpu.VMEM((NX, 1, ROWS), jnp.float32),
            pltpu.VMEM((NX, 1, ROWS), jnp.float32),
            pltpu.VMEM((NX, HD, ROWS), jnp.float32),
            pltpu.SMEM((ENTRIES + PAIR,), jnp.int32),
            pltpu.SemaphoreType.DMA((NY + 2,)),
        ],
        compiler_params=pltpu.CompilerParams(vmem_limit_bytes=16 << 20),
        name="attend_home" if home else "attend_other",
    )(x, core, lists, new_kv, own, *shards[1:], asked)


def combine_kernel(one, two, out):
    for g in range(NX):
        levels = [join_level(part[g, pl.ds(HD, STATS), :]) for part in (one, two)]
        top = jnp.maximum(*levels)
        shares = [jnp.exp2(level - top) for level in levels]
        whole = shares[0] + shares[1]
        inverse = 1.0 / whole
        rows = [part[g, pl.ds(0, HD), :].astype(jnp.float32) * (share * inverse) for part, share in zip((one, two), shares)]
        out[g, pl.ds(0, HD), :] = (rows[0] + rows[1]).astype(jnp.bfloat16)
        out[g, pl.ds(HD, STATS), :] = split_level(top + jnp.log2(whole))


def combine(one, two):
    vmem = pl.BlockSpec(memory_space=pltpu.VMEM)
    return pl.pallas_call(
        combine_kernel,
        out_shape=jax.ShapeDtypeStruct(one.shape, one.dtype),
        in_specs=[vmem, vmem],
        out_specs=vmem,
        compiler_params=pltpu.CompilerParams(vmem_limit_bytes=8 << 20),
        name="combine",
    )(one, two)


def project_kernel(parts, weight, out, attended):
    @pl.when(pl.program_id(0) == 0)
    def _():
        levels = []
        for i in range(NX):
            levels.append(join_level(parts[i, pl.ds(HD, STATS), :]))
        top = levels[0]
        for level in levels[1:]:
            top = jnp.maximum(top, level)
        shares = [jnp.exp2(level - top) for level in levels]
        whole = shares[0]
        for share in shares[1:]:
            whole = whole + share
        for h in range(PER):
            columns = pl.ds(h * TOK, TOK)
            mixed = jnp.zeros((HD, TOK), jnp.float32)
            for i in range(NX):
                mixed = mixed + parts[i, pl.ds(0, HD), columns].astype(jnp.float32) * (shares[i] / whole)[:, h * TOK:(h + 1) * TOK]
            attended[:, h * HD:(h + 1) * HD] = jnp.transpose(mixed).astype(jnp.bfloat16)

    out[...] = jnp.dot(attended[...], weight[...], preferred_element_type=jnp.float32).astype(jnp.bfloat16)


def project(parts, weight):
    width = weight.shape[1]
    step = 1024
    return pl.pallas_call(
        project_kernel,
        out_shape=jax.ShapeDtypeStruct((TOK, width), jnp.bfloat16),
        grid=(width // step,),
        in_specs=[
            pl.BlockSpec((NX, HD + STATS, ROWS), lambda n: (0, 0, 0)),
            pl.BlockSpec((ROWS, step), lambda n: (0, n)),
        ],
        out_specs=pl.BlockSpec((TOK, step), lambda n: (0, n)),
        scratch_shapes=[pltpu.VMEM((TOK, ROWS), jnp.bfloat16)],
        compiler_params=pltpu.CompilerParams(vmem_limit_bytes=16 << 20),
        name="project",
    )(parts, weight)


def spread(cache, queries):
    def shift(a, hops):
        pairs = [(y * NC + c, (y + hops * (1 - 2 * c)) % NY * NC + c) for y in range(NY) for c in range(NC)]
        return lax.ppermute(a, ("y", "c"), pairs)

    behind2, ahead2 = shift(cache, 2), shift(cache, -2)
    behind1, ahead1 = shift(cache, 1), shift(cache, -1)
    across, behind3, ahead3 = shift(behind2, 2), shift(behind2, 1), shift(ahead2, -1)
    same = lax.all_gather(queries, "x", axis=0)
    later = (behind1, ahead1, across, behind3, ahead3)
    same, behind1, ahead1, across, behind3, ahead3 = lax.optimization_barrier((same, *later))
    swapped = lax.ppermute(same, "c", [(0, 1), (1, 0)])
    return [cache, ahead1, ahead2, ahead3, across, behind3, behind2, behind1], [same, swapped]


def local(queries, new_kv, cache, block_owner, block_slot, prefix_blocks, out_weight):
    x, y, c = (lax.axis_index(name).reshape(1) for name in ("x", "y", "c"))
    shards, asked = spread(cache, queries)
    lists = block_lists(x, y, c, prefix_blocks, block_owner, block_slot)
    other = attend(False, x, 1 - c, lists, new_kv, asked[1], shards)
    lists, other = lax.optimization_barrier((lists, other))
    returned = lax.ppermute(other, "c", [(0, 1), (1, 0)])
    parts = combine(attend(True, x, c, lists, new_kv, asked[0], shards), returned)
    parts = lax.all_to_all(parts, "x", split_axis=0, concat_axis=0, tiled=True)
    partial = project(parts, out_weight).reshape(NZ, TOK // NZ, -1)
    arrived = lax.all_to_all(partial, "z", split_axis=0, concat_axis=0, tiled=True)
    return jnp.sum(arrived.astype(jnp.float32), axis=0).astype(jnp.bfloat16)


def solution(mesh):
    fine = Mesh(mesh.devices.reshape(NX, NY, NC, NZ), ("x", "y", "c", "z"))
    replica = ("x", "y", "c")
    placed = (
        P(replica, "z"),
        P(None, replica, "z"),
        P(replica, None, None, "z"),
        P(),
        P(),
        P(),
        P("z", None),
    )
    return jax.shard_map(
        local, mesh=fine, in_specs=placed, out_specs=P(("x", "y", "c", "z"), None), check_vma=False
    )
```

```python
import functools
import math

import jax
import jax.numpy as jnp
from jax import lax
from jax.experimental import pallas as pl
from jax.experimental.pallas import tpu as pltpu
from jax.sharding import Mesh, PartitionSpec as P

HQ = 32
KVH = 8
HD = 128
BLOCK = 64
MAXB = 64
NX, NY, NC, NZ = 4, 8, 2, 8
GROUP = NX * NC
PER = HQ // KVH
TOK = 128
ROWS = PER * TOK
SLOTS = 8
CAP = 2
LIST = NY * CAP
TILE = 4
ENTRIES = NX * LIST // TILE
PAIR = 2
STATS = 16
NEGATIVE = -1e30
FLOOR = -1e29
LOG2 = HD ** (-0.5) * math.log2(math.e)


def contract(a, b, da, db):
    return lax.dot_general(a, b, (((da,), (db,)), ((), ())), preferred_element_type=jnp.float32)


def lists_kernel(x, y, c, lengths, owners, slots, lists):
    rows = [(g // NC * NY + y[0]) * NC + g % NC for g in range(GROUP)]
    owner = jnp.concatenate([owners[pl.ds(r, 1), :] for r in rows], axis=0)
    slot = jnp.concatenate([slots[pl.ds(r, 1), :] for r in rows], axis=0)
    length = jnp.concatenate([jnp.full((1, MAXB), lengths[r], jnp.int32) for r in rows], axis=0)
    place = lax.broadcasted_iota(jnp.int32, (GROUP, MAXB), 1)
    mine = (owner // (NY * NC) == x[0]) & (owner % NC == c[0]) & (place < length)
    code = ((owner // NC - y[0]) * (1 - 2 * c[0]) + 2 * NY) % NY * SLOTS + slot
    earlier = lax.broadcasted_iota(jnp.int32, (MAXB, MAXB), 0) < lax.broadcasted_iota(jnp.int32, (MAXB, MAXB), 1)
    flags = mine.astype(jnp.float32)
    ranks = jnp.dot(flags, earlier.astype(jnp.float32), preferred_element_type=jnp.float32)
    lane = lax.broadcasted_iota(jnp.int32, (GROUP, HD), 1)
    table = jnp.where(lane == LIST, jnp.sum(flags, axis=1, keepdims=True), 0.0)
    code = jnp.where(mine, code.astype(jnp.float32), 0.0)
    for k in range(LIST):
        entry = jnp.sum(jnp.where(ranks == k, code, 0.0), axis=1, keepdims=True)
        table = jnp.where(lane == k, entry, table)
    lists[...] = table.astype(jnp.int32)


def block_lists(x, y, c, lengths, owners, slots):
    vmem, smem = pl.BlockSpec(memory_space=pltpu.VMEM), pl.BlockSpec(memory_space=pltpu.SMEM)
    return pl.pallas_call(
        lists_kernel,
        out_shape=pltpu.VMEM((GROUP, HD), jnp.int32),
        in_specs=[smem] * 4 + [vmem] * 2,
        out_specs=vmem,
        compiler_params=pltpu.CompilerParams(vmem_limit_bytes=4 << 20),
        name="block_lists",
    )(x, y, c, lengths, *(pltpu.with_memory_space_constraint(a, pltpu.HBM) for a in (owners, slots)))


def split_level(level):
    high = level.astype(jnp.bfloat16).astype(jnp.float32)
    middle = (level - high).astype(jnp.bfloat16).astype(jnp.float32)
    row = lax.broadcasted_iota(jnp.int32, (STATS, ROWS), 0)
    stats = jnp.where(row == 0, high, jnp.where(row == 1, middle, jnp.where(row == 2, level - high - middle, 0.0)))
    return stats.astype(jnp.bfloat16)


def join_level(stats):
    stats = stats.astype(jnp.float32)
    return stats[0:1] + stats[1:2] + stats[2:3]


def attend_kernel(home, x, core, lists, queries, *rest):
    if home:
        held, new_kv, out, fresh, peak, total, weighted, order, sems = rest
        copies = [pltpu.make_async_copy(new_kv, fresh, sems.at[0])]
    else:
        shards, (out, held, peak, total, weighted, order, sems) = rest[:NY], rest[NY:]
        copies = [pltpu.make_async_copy(shards[s], held.at[pl.ds(s * SLOTS, SLOTS)], sems.at[s]) for s in range(NY)]
    for copy in copies:
        copy.start()

    def heads(g):
        q = queries[g]
        return jnp.concatenate([q[:, h * HD:(h + 1) * HD] for h in range(PER)], axis=0)

    def reduce(scores, values):
        top = jnp.maximum(jnp.max(scores, axis=0, keepdims=True), FLOOR)
        weights = jnp.exp2((scores - top) * LOG2)
        return top, jnp.sum(weights, axis=0, keepdims=True), contract(values, weights.astype(jnp.bfloat16), 0, 0)

    def merge(g, top, amount, product):
        highest = jnp.maximum(peak[g], top)
        before, now = jnp.exp2((peak[g] - highest) * LOG2), jnp.exp2((top - highest) * LOG2)
        peak[g] = highest
        total[g] = total[g] * before + amount * now
        weighted[g] = weighted[g] * before + product * now

    def append(entry, used):
        g, j = entry % NX, entry // NX
        wanted = lists[g * NC + core[0], LIST] > j * TILE

        @pl.when(wanted)
        def _():
            order[used] = entry

        return used + wanted.astype(jnp.int32)

    peak[...] = jnp.full(peak.shape, FLOOR, jnp.float32)
    total[...] = jnp.zeros(total.shape, jnp.float32)
    weighted[...] = jnp.zeros(weighted.shape, jnp.float32)
    used = lax.fori_loop(0, ENTRIES, append, 0)
    for p in range(PAIR):
        order[used + p] = ENTRIES

    for copy in copies:
        copy.wait()
    if home:
        scores = contract(fresh[0], heads(x[0]), 1, 1)
        key = lax.broadcasted_iota(jnp.int32, (TOK, ROWS), 0)
        token = lax.broadcasted_iota(jnp.int32, (TOK, ROWS), 1) % TOK
        merge(x[0], *reduce(jnp.where(key <= token, scores, NEGATIVE), fresh[1]))

    def some_tiles(i, carry):
        results = []
        for p in range(PAIR):
            entry = order[i * PAIR + p]
            valid = entry < ENTRIES
            g, j = entry % NX, jnp.where(valid, entry // NX, 0)
            row = g * NC + core[0]
            left = jnp.where(valid, (lists[row, LIST] - j * TILE) * BLOCK, 0)
            ids = [lists[row, j * TILE + k] for k in range(TILE)]
            keys = jnp.concatenate([held[b, 0] for b in ids], axis=0)
            values = jnp.concatenate([held[b, 1] for b in ids], axis=0)
            scores = contract(keys, heads(g), 1, 1)
            place = lax.broadcasted_iota(jnp.int32, scores.shape, 0)
            results.append((g, *reduce(jnp.where(place < left, scores, NEGATIVE), values)))
        for result in results:
            merge(*result)
        return carry

    lax.fori_loop(0, (used + PAIR - 1) // PAIR, some_tiles, 0)

    def finish(g, carry):
        filled = total[g] > 0.0
        safe = jnp.where(filled, total[g], 1.0)
        level = jnp.where(filled, peak[g] * LOG2 + jnp.log2(safe), NEGATIVE)
        out[g, pl.ds(0, HD), :] = (weighted[g] * (1.0 / safe)).astype(jnp.bfloat16)
        out[g, pl.ds(HD, STATS), :] = split_level(level)
        return carry

    lax.fori_loop(0, NX, finish, 0)


def attend(home, x, core, lists, asked, arrays):
    vmem, smem, free = (pl.BlockSpec(memory_space=m) for m in (pltpu.VMEM, pltpu.SMEM, pl.ANY))
    result = jax.ShapeDtypeStruct((NX, HD + STATS, ROWS), jnp.bfloat16)
    blocks = (NY * SLOTS, 2, BLOCK, HD)
    return pl.pallas_call(
        functools.partial(attend_kernel, home),
        out_shape=result if home else [result, pltpu.VMEM(blocks, jnp.bfloat16)],
        in_specs=[smem, smem, smem, vmem] + ([vmem, free] if home else [free] * NY),
        out_specs=vmem if home else [vmem, vmem],
        scratch_shapes=([pltpu.VMEM((2, TOK, HD), jnp.bfloat16)] if home else [])
        + [
            pltpu.VMEM((NX, 1, ROWS), jnp.float32),
            pltpu.VMEM((NX, 1, ROWS), jnp.float32),
            pltpu.VMEM((NX, HD, ROWS), jnp.float32),
            pltpu.SMEM((ENTRIES + PAIR,), jnp.int32),
            pltpu.SemaphoreType.DMA((NY,)),
        ],
        compiler_params=pltpu.CompilerParams(vmem_limit_bytes=16 << 20),
        name="attend_home" if home else "attend_other",
    )(x, core, lists, asked, *arrays)


def combine_kernel(one, two, out):
    for g in range(NX):
        levels = [join_level(part[g, pl.ds(HD, STATS), :]) for part in (one, two)]
        top = jnp.maximum(*levels)
        shares = [jnp.exp2(level - top) for level in levels]
        whole = shares[0] + shares[1]
        inverse = 1.0 / whole
        rows = [part[g, pl.ds(0, HD), :].astype(jnp.float32) * (share * inverse) for part, share in zip((one, two), shares)]
        out[g, pl.ds(0, HD), :] = (rows[0] + rows[1]).astype(jnp.bfloat16)
        out[g, pl.ds(HD, STATS), :] = split_level(top + jnp.log2(whole))


def combine(one, two):
    vmem = pl.BlockSpec(memory_space=pltpu.VMEM)
    return pl.pallas_call(
        combine_kernel,
        out_shape=jax.ShapeDtypeStruct(one.shape, one.dtype),
        in_specs=[vmem, vmem],
        out_specs=vmem,
        compiler_params=pltpu.CompilerParams(vmem_limit_bytes=8 << 20),
        name="combine",
    )(one, two)


def project_kernel(parts, weight, out, attended):
    @pl.when(pl.program_id(0) == 0)
    def _():
        levels = []
        for i in range(NX):
            levels.append(join_level(parts[i, pl.ds(HD, STATS), :]))
        top = levels[0]
        for level in levels[1:]:
            top = jnp.maximum(top, level)
        shares = [jnp.exp2(level - top) for level in levels]
        whole = shares[0]
        for share in shares[1:]:
            whole = whole + share
        for h in range(PER):
            columns = pl.ds(h * TOK, TOK)
            mixed = jnp.zeros((HD, TOK), jnp.float32)
            for i in range(NX):
                mixed = mixed + parts[i, pl.ds(0, HD), columns].astype(jnp.float32) * (shares[i] / whole)[:, h * TOK:(h + 1) * TOK]
            attended[:, h * HD:(h + 1) * HD] = jnp.transpose(mixed).astype(jnp.bfloat16)

    out[...] = jnp.dot(attended[...], weight[...], preferred_element_type=jnp.float32).astype(jnp.bfloat16)


def project(parts, weight):
    width = weight.shape[1]
    step = 1024
    return pl.pallas_call(
        project_kernel,
        out_shape=jax.ShapeDtypeStruct((TOK, width), jnp.bfloat16),
        grid=(width // step,),
        in_specs=[
            pl.BlockSpec((NX, HD + STATS, ROWS), lambda n: (0, 0, 0)),
            pl.BlockSpec((ROWS, step), lambda n: (0, n)),
        ],
        out_specs=pl.BlockSpec((TOK, step), lambda n: (0, n)),
        scratch_shapes=[pltpu.VMEM((TOK, ROWS), jnp.bfloat16)],
        compiler_params=pltpu.CompilerParams(vmem_limit_bytes=16 << 20),
        name="project",
    )(parts, weight)


def spread(cache, queries):
    def shift(a, hops):
        pairs = [(y * NC + c, (y + hops * (1 - 2 * c)) % NY * NC + c) for y in range(NY) for c in range(NC)]
        return lax.ppermute(a, ("y", "c"), pairs)

    behind2, ahead2 = shift(cache, 2), shift(cache, -2)
    behind1, ahead1 = shift(cache, 1), shift(cache, -1)
    across, behind3, ahead3 = shift(behind2, 2), shift(behind2, 1), shift(ahead2, -1)
    same = lax.all_gather(queries, "x", axis=0)
    later = (behind1, ahead1, across, behind3, ahead3)
    same, behind1, ahead1, across, behind3, ahead3 = lax.optimization_barrier((same, *later))
    swapped = lax.ppermute(same, "c", [(0, 1), (1, 0)])
    return [cache, ahead1, ahead2, ahead3, across, behind3, behind2, behind1], [same, swapped]


def local(queries, new_kv, cache, block_owner, block_slot, prefix_blocks, out_weight):
    x, y, c = (lax.axis_index(name).reshape(1) for name in ("x", "y", "c"))
    shards, asked = spread(cache, queries)
    lists = block_lists(x, y, c, prefix_blocks, block_owner, block_slot)
    new_kv, own = (pltpu.with_memory_space_constraint(a, pltpu.HBM) for a in (new_kv, shards[0]))
    other, held = attend(False, x, 1 - c, lists, asked[1], [own, *shards[1:]])
    returned = lax.ppermute(other, "c", [(0, 1), (1, 0)])
    parts = combine(attend(True, x, c, lists, asked[0], [held, new_kv]), returned)
    parts = lax.all_to_all(parts, "x", split_axis=0, concat_axis=0, tiled=True)
    partial = project(parts, out_weight).reshape(NZ, TOK // NZ, -1)
    arrived = lax.all_to_all(partial, "z", split_axis=0, concat_axis=0, tiled=True)
    return jnp.sum(arrived.astype(jnp.float32), axis=0).astype(jnp.bfloat16)


def solution(mesh):
    fine = Mesh(mesh.devices.reshape(NX, NY, NC, NZ), ("x", "y", "c", "z"))
    replica = ("x", "y", "c")
    placed = (
        P(replica, "z"),
        P(None, replica, "z"),
        P(replica, None, None, "z"),
        P(),
        P(),
        P(),
        P("z", None),
    )
    return jax.shard_map(
        local, mesh=fine, in_specs=placed, out_specs=P(("x", "y", "c", "z"), None), check_vma=False
    )
```

```python
import functools
import math

import jax
import jax.numpy as jnp
from jax import lax
from jax.experimental import pallas as pl
from jax.experimental.pallas import tpu as pltpu
from jax.sharding import Mesh, PartitionSpec as P

HQ = 32
KVH = 8
HD = 128
BLOCK = 64
MAXB = 64
NX, NY, NC, NZ = 4, 8, 2, 8
GROUP = NX * NC
PER = HQ // KVH
TOK = 128
ROWS = PER * TOK
SLOTS = 8
CAP = 2
LIST = NY * CAP
TILE = 4
ENTRIES = NX * LIST // TILE
PAIR = 2
STATS = 16
NEGATIVE = -1e30
FLOOR = -1e29
LOG2 = HD ** (-0.5) * math.log2(math.e)


def contract(a, b, da, db):
    return lax.dot_general(a, b, (((da,), (db,)), ((), ())), preferred_element_type=jnp.float32)


def lists_kernel(x, y, c, lengths, owners, slots, lists):
    rows = [(g // NC * NY + y[0]) * NC + g % NC for g in range(GROUP)]
    owner = jnp.concatenate([owners[pl.ds(r, 1), :] for r in rows], axis=0)
    slot = jnp.concatenate([slots[pl.ds(r, 1), :] for r in rows], axis=0)
    length = jnp.concatenate([jnp.full((1, MAXB), lengths[r], jnp.int32) for r in rows], axis=0)
    place = lax.broadcasted_iota(jnp.int32, (GROUP, MAXB), 1)
    mine = (owner // (NY * NC) == x[0]) & (owner % NC == c[0]) & (place < length)
    code = ((owner // NC - y[0]) * (1 - 2 * c[0]) + 2 * NY) % NY * SLOTS + slot
    earlier = lax.broadcasted_iota(jnp.int32, (MAXB, MAXB), 0) < lax.broadcasted_iota(jnp.int32, (MAXB, MAXB), 1)
    flags = mine.astype(jnp.float32)
    ranks = jnp.dot(flags, earlier.astype(jnp.float32), preferred_element_type=jnp.float32)
    lane = lax.broadcasted_iota(jnp.int32, (GROUP, HD), 1)
    table = jnp.where(lane == LIST, jnp.sum(flags, axis=1, keepdims=True), 0.0)
    code = jnp.where(mine, code.astype(jnp.float32), 0.0)
    for k in range(LIST):
        entry = jnp.sum(jnp.where(ranks == k, code, 0.0), axis=1, keepdims=True)
        table = jnp.where(lane == k, entry, table)
    lists[...] = table.astype(jnp.int32)


def block_lists(x, y, c, lengths, owners, slots):
    vmem, smem = pl.BlockSpec(memory_space=pltpu.VMEM), pl.BlockSpec(memory_space=pltpu.SMEM)
    return pl.pallas_call(
        lists_kernel,
        out_shape=pltpu.VMEM((GROUP, HD), jnp.int32),
        in_specs=[smem] * 4 + [vmem] * 2,
        out_specs=vmem,
        compiler_params=pltpu.CompilerParams(vmem_limit_bytes=4 << 20),
        name="block_lists",
    )(x, y, c, *(pltpu.with_memory_space_constraint(a, pltpu.HBM) for a in (lengths, owners, slots)))


def split_level(level):
    high = level.astype(jnp.bfloat16).astype(jnp.float32)
    middle = (level - high).astype(jnp.bfloat16).astype(jnp.float32)
    row = lax.broadcasted_iota(jnp.int32, (STATS, ROWS), 0)
    stats = jnp.where(row == 0, high, jnp.where(row == 1, middle, jnp.where(row == 2, level - high - middle, 0.0)))
    return stats.astype(jnp.bfloat16)


def join_level(stats):
    stats = stats.astype(jnp.float32)
    return stats[0:1] + stats[1:2] + stats[2:3]


def attend_kernel(home, x, core, lists, queries, *rest):
    if home:
        held, new_kv, out, fresh, peak, total, weighted, order, sems = rest
        copies = [pltpu.make_async_copy(new_kv, fresh, sems.at[0])]
    else:
        shards, (out, held, peak, total, weighted, order, sems) = rest[:NY], rest[NY:]
        copies = [pltpu.make_async_copy(shards[s], held.at[pl.ds(s * SLOTS, SLOTS)], sems.at[s]) for s in range(NY)]
    for copy in copies:
        copy.start()

    def heads(g):
        q = queries[g]
        return jnp.concatenate([q[:, h * HD:(h + 1) * HD] for h in range(PER)], axis=0)

    def reduce(scores, values):
        top = jnp.maximum(jnp.max(scores, axis=0, keepdims=True), FLOOR)
        weights = jnp.exp2((scores - top) * LOG2)
        return top, jnp.sum(weights, axis=0, keepdims=True), contract(values, weights.astype(jnp.bfloat16), 0, 0)

    def merge(g, top, amount, product):
        highest = jnp.maximum(peak[g], top)
        before, now = jnp.exp2((peak[g] - highest) * LOG2), jnp.exp2((top - highest) * LOG2)
        peak[g] = highest
        total[g] = total[g] * before + amount * now
        weighted[g] = weighted[g] * before + product * now

    def append(entry, used):
        g, j = entry % NX, entry // NX
        wanted = lists[g * NC + core[0], LIST] > j * TILE

        @pl.when(wanted)
        def _():
            order[used] = entry

        return used + wanted.astype(jnp.int32)

    peak[...] = jnp.full(peak.shape, FLOOR, jnp.float32)
    total[...] = jnp.zeros(total.shape, jnp.float32)
    weighted[...] = jnp.zeros(weighted.shape, jnp.float32)
    used = lax.fori_loop(0, ENTRIES, append, 0)
    for p in range(PAIR):
        order[used + p] = ENTRIES

    for copy in copies:
        copy.wait()
    if home:
        scores = contract(fresh[0], heads(x[0]), 1, 1)
        key = lax.broadcasted_iota(jnp.int32, (TOK, ROWS), 0)
        token = lax.broadcasted_iota(jnp.int32, (TOK, ROWS), 1) % TOK
        merge(x[0], *reduce(jnp.where(key <= token, scores, NEGATIVE), fresh[1]))

    def some_tiles(i, carry):
        results = []
        for p in range(PAIR):
            entry = order[i * PAIR + p]
            valid = entry < ENTRIES
            g, j = entry % NX, jnp.where(valid, entry // NX, 0)
            row = g * NC + core[0]
            left = jnp.where(valid, (lists[row, LIST] - j * TILE) * BLOCK, 0)
            ids = [lists[row, j * TILE + k] for k in range(TILE)]
            keys = jnp.concatenate([held[b, 0] for b in ids], axis=0)
            values = jnp.concatenate([held[b, 1] for b in ids], axis=0)
            scores = contract(keys, heads(g), 1, 1)
            place = lax.broadcasted_iota(jnp.int32, scores.shape, 0)
            results.append((g, *reduce(jnp.where(place < left, scores, NEGATIVE), values)))
        for result in results:
            merge(*result)
        return carry

    lax.fori_loop(0, (used + PAIR - 1) // PAIR, some_tiles, 0)

    def finish(g, carry):
        filled = total[g] > 0.0
        safe = jnp.where(filled, total[g], 1.0)
        level = jnp.where(filled, peak[g] * LOG2 + jnp.log2(safe), NEGATIVE)
        out[g, pl.ds(0, HD), :] = (weighted[g] * (1.0 / safe)).astype(jnp.bfloat16)
        out[g, pl.ds(HD, STATS), :] = split_level(level)
        return carry

    lax.fori_loop(0, NX, finish, 0)


def attend(home, x, core, lists, asked, arrays):
    vmem, smem, free = (pl.BlockSpec(memory_space=m) for m in (pltpu.VMEM, pltpu.SMEM, pl.ANY))
    result = jax.ShapeDtypeStruct((NX, HD + STATS, ROWS), jnp.bfloat16)
    blocks = (NY * SLOTS, 2, BLOCK, HD)
    return pl.pallas_call(
        functools.partial(attend_kernel, home),
        out_shape=result if home else [result, pltpu.VMEM(blocks, jnp.bfloat16)],
        in_specs=[smem, smem, smem, vmem] + ([vmem, free] if home else [free] * NY),
        out_specs=vmem if home else [vmem, vmem],
        scratch_shapes=([pltpu.VMEM((2, TOK, HD), jnp.bfloat16)] if home else [])
        + [
            pltpu.VMEM((NX, 1, ROWS), jnp.float32),
            pltpu.VMEM((NX, 1, ROWS), jnp.float32),
            pltpu.VMEM((NX, HD, ROWS), jnp.float32),
            pltpu.SMEM((ENTRIES + PAIR,), jnp.int32),
            pltpu.SemaphoreType.DMA((NY,)),
        ],
        compiler_params=pltpu.CompilerParams(vmem_limit_bytes=16 << 20),
        name="attend_home" if home else "attend_other",
    )(x, core, lists, asked, *arrays)


def combine_kernel(one, two, out):
    for g in range(NX):
        levels = [join_level(part[g, pl.ds(HD, STATS), :]) for part in (one, two)]
        top = jnp.maximum(*levels)
        shares = [jnp.exp2(level - top) for level in levels]
        whole = shares[0] + shares[1]
        inverse = 1.0 / whole
        rows = [part[g, pl.ds(0, HD), :].astype(jnp.float32) * (share * inverse) for part, share in zip((one, two), shares)]
        out[g, pl.ds(0, HD), :] = (rows[0] + rows[1]).astype(jnp.bfloat16)
        out[g, pl.ds(HD, STATS), :] = split_level(top + jnp.log2(whole))


def combine(one, two):
    vmem = pl.BlockSpec(memory_space=pltpu.VMEM)
    return pl.pallas_call(
        combine_kernel,
        out_shape=jax.ShapeDtypeStruct(one.shape, one.dtype),
        in_specs=[vmem, vmem],
        out_specs=vmem,
        compiler_params=pltpu.CompilerParams(vmem_limit_bytes=8 << 20),
        name="combine",
    )(one, two)


def project_kernel(parts, weight, out, attended):
    @pl.when(pl.program_id(0) == 0)
    def _():
        levels = []
        for i in range(NX):
            levels.append(join_level(parts[i, pl.ds(HD, STATS), :]))
        top = levels[0]
        for level in levels[1:]:
            top = jnp.maximum(top, level)
        shares = [jnp.exp2(level - top) for level in levels]
        whole = shares[0]
        for share in shares[1:]:
            whole = whole + share
        for h in range(PER):
            columns = pl.ds(h * TOK, TOK)
            mixed = jnp.zeros((HD, TOK), jnp.float32)
            for i in range(NX):
                mixed = mixed + parts[i, pl.ds(0, HD), columns].astype(jnp.float32) * (shares[i] / whole)[:, h * TOK:(h + 1) * TOK]
            attended[:, h * HD:(h + 1) * HD] = jnp.transpose(mixed).astype(jnp.bfloat16)

    out[...] = jnp.dot(attended[...], weight[...], preferred_element_type=jnp.float32).astype(jnp.bfloat16)


def project(parts, weight):
    width = weight.shape[1]
    step = 1024
    return pl.pallas_call(
        project_kernel,
        out_shape=jax.ShapeDtypeStruct((TOK, width), jnp.bfloat16),
        grid=(width // step,),
        in_specs=[
            pl.BlockSpec((NX, HD + STATS, ROWS), lambda n: (0, 0, 0)),
            pl.BlockSpec((ROWS, step), lambda n: (0, n)),
        ],
        out_specs=pl.BlockSpec((TOK, step), lambda n: (0, n)),
        scratch_shapes=[pltpu.VMEM((TOK, ROWS), jnp.bfloat16)],
        compiler_params=pltpu.CompilerParams(vmem_limit_bytes=16 << 20),
        name="project",
    )(parts, weight)


def spread(cache, queries):
    def shift(a, hops):
        pairs = [(y * NC + c, (y + hops * (1 - 2 * c)) % NY * NC + c) for y in range(NY) for c in range(NC)]
        return lax.ppermute(a, ("y", "c"), pairs)

    behind2, ahead2 = shift(cache, 2), shift(cache, -2)
    behind1, ahead1 = shift(cache, 1), shift(cache, -1)
    across, behind3, ahead3 = shift(behind2, 2), shift(behind2, 1), shift(ahead2, -1)
    same = lax.all_gather(queries, "x", axis=0)
    later = (behind1, ahead1, across, behind3, ahead3)
    same, behind1, ahead1, across, behind3, ahead3 = lax.optimization_barrier((same, *later))
    swapped = lax.ppermute(same, "c", [(0, 1), (1, 0)])
    return [cache, ahead1, ahead2, ahead3, across, behind3, behind2, behind1], [same, swapped]


def local(queries, new_kv, cache, block_owner, block_slot, prefix_blocks, out_weight):
    x, y, c = (lax.axis_index(name).reshape(1) for name in ("x", "y", "c"))
    shards, asked = spread(cache, queries)
    lists = block_lists(x, y, c, prefix_blocks, block_owner, block_slot)
    new_kv, own = (pltpu.with_memory_space_constraint(a, pltpu.HBM) for a in (new_kv, shards[0]))
    other, held = attend(False, x, 1 - c, lists, asked[1], [own, *shards[1:]])
    returned = lax.ppermute(other, "c", [(0, 1), (1, 0)])
    parts = combine(attend(True, x, c, lists, asked[0], [held, new_kv]), returned)
    parts = lax.all_to_all(parts, "x", split_axis=0, concat_axis=0, tiled=True)
    partial = project(parts, out_weight).reshape(NZ, TOK // NZ, -1)
    arrived = lax.all_to_all(partial, "z", split_axis=0, concat_axis=0, tiled=True)
    return jnp.sum(arrived.astype(jnp.float32), axis=0).astype(jnp.bfloat16)


def solution(mesh):
    fine = Mesh(mesh.devices.reshape(NX, NY, NC, NZ), ("x", "y", "c", "z"))
    replica = ("x", "y", "c")
    placed = (
        P(replica, "z"),
        P(None, replica, "z"),
        P(replica, None, None, "z"),
        P(),
        P(),
        P(),
        P("z", None),
    )
    return jax.shard_map(
        local, mesh=fine, in_specs=placed, out_specs=P(("x", "y", "c", "z"), None), check_vma=False
    )
```
